32 devices in a mesh: ctx: 8 (over y, x, core), head: 4 (over z).
Axes of the slice: x: 2, y: 2, z: 4, core: 2. Of those that a mesh axis runs over, the one named last changes fastest.
Arguments:
- lin_q: bfloat16 [2048, 8192], P('ctx', 'head'), may hold values from -4 to 4
- lin_k: bfloat16 [2048, 8192], P('ctx', 'head'), may hold values from -4 to 4
- lin_v: bfloat16 [2048, 8192], P('ctx', 'head'), may hold values from -6 to 6
- log_decay: float32 [64, 2048], P('head', 'ctx'), may hold values from -1 to 0
- lin_gain: float32 [8192], P('head'), may hold values from 0.1 to 1.9
- soft_q: bfloat16 [2048, 8192], P(('ctx', 'head')), may hold values from -200 to 200
- soft_kv: bfloat16 [2048, 2048], P(('ctx', 'head')), may hold values from -8 to 8
Outputs:
- lin_out: bfloat16 [2048, 8192], P('ctx', 'head')
- soft_out: bfloat16 [2048, 8192], P(('ctx', 'head'))
The draws below stay inside these ranges and needn't reach their ends.
All inputs are finite; a program needn't handle non-finite values.
Results may differ from the reference program's by a relative error of at most 0.013.
Values may be sent and summed in bfloat16 or wider, within the bound.
A program may use at most 64 MiB of HBM per device.

```python
import math
import jax
import jax.numpy as jnp
from jax import lax

HEAD_COUNT = 64
KVH = 8
DH = 128
BLOCK = 256
SEQUENCE_LENGTH = 2048


def draw_log_decay(key, part):
    key_matrix = jax.random.split(jax.random.fold_in(key, 7), 6)
    share = 0.5
    fast = jax.random.uniform(key_matrix[0], (HEAD_COUNT,)) < share
    fast_rate = jnp.exp(jax.random.uniform(key_matrix[1], (HEAD_COUNT,), minval=math.log(0.05), maxval=math.log(0.1)))
    slow_rate = jnp.exp(jax.random.uniform(key_matrix[2], (HEAD_COUNT,), minval=math.log(0.02), maxval=math.log(0.3))) * math.log(10.0) / SEQUENCE_LENGTH
    decay_speed = jnp.where(fast, fast_rate, slow_rate)[:, None]
    decay_factor = jnp.exp(jax.random.uniform(key_matrix[3], (HEAD_COUNT, SEQUENCE_LENGTH // BLOCK), minval=math.log(0.5), maxval=math.log(1.5)))
    decay_factor = jnp.repeat(decay_factor, BLOCK, axis=1)
    sudden_decay = jax.random.uniform(key_matrix[4], (HEAD_COUNT, SEQUENCE_LENGTH)) < 3.0 / SEQUENCE_LENGTH
    sudden_log_decay = jnp.log(jax.random.uniform(key_matrix[5], (HEAD_COUNT, SEQUENCE_LENGTH), minval=0.5, maxval=0.8))
    value_rows = -decay_speed * decay_factor + jnp.where(sudden_decay, sudden_log_decay, 0.0)
    return value_rows.astype(jnp.float32)


def soft_parts(key):
    key_matrix = jax.random.split(jax.random.fold_in(key, 11), 3)
    queries = jax.random.normal(key_matrix[0], (SEQUENCE_LENGTH, HEAD_COUNT, DH), jnp.float32)
    keyrows = jax.random.normal(key_matrix[1], (SEQUENCE_LENGTH, KVH, DH), jnp.float32)
    value_rows = jax.random.normal(key_matrix[2], (SEQUENCE_LENGTH, KVH, DH), jnp.float32)
    queries = jnp.clip(queries, -200.0, 200.0)
    keyrows = jnp.clip(keyrows, -8.0, 8.0)
    value_rows = jnp.clip(value_rows, -8.0, 8.0)
    joined = jnp.stack([keyrows, value_rows], axis=2).reshape(SEQUENCE_LENGTH, KVH * 2 * DH)
    return (queries.reshape(SEQUENCE_LENGTH, HEAD_COUNT * DH), joined)


def draw_soft_q(key, part):
    queries, joined = soft_parts(key)
    return queries.astype(jnp.bfloat16)


def draw_soft_kv(key, part):
    queries, joined = soft_parts(key)
    return joined.astype(jnp.bfloat16)


def block_scale(stream_key, dims, shards, low, top_value):
    gain, own = 1.0, jax.random.fold_in(stream_key, 6)
    for position, blocks in shards:
        draws = jnp.exp(jax.random.uniform(jax.random.fold_in(own, position), (blocks,), jnp.float32, low / len(shards), top_value / len(shards)))
        gain = gain * jnp.repeat(draws, dims[position] // blocks).reshape([-1 if axis == position else 1 for axis in range(len(dims))])
    return gain


def gaussian(rng, extent, scale, reach, cuts=(), dtype=jnp.bfloat16):
    entries = jax.random.normal(rng, extent, jnp.float32) * scale
    if len(cuts) > 0:
        entries = block_scale(rng, extent, cuts, -0.22, 0.18) * entries
    return jnp.clip(entries, min=-reach, max=reach).astype(dtype)


def setup_inputs(seed: int = 0) -> dict:
    arg_keys = jax.random.split(jax.random.key(seed), 8)
    return {
        "lin_q": gaussian(arg_keys[0], (SEQUENCE_LENGTH, HEAD_COUNT * DH), 0.3, 4.0, ((0, 8), (1, 4))),
        "lin_k": gaussian(arg_keys[1], (SEQUENCE_LENGTH, HEAD_COUNT * DH), 0.3, 4.0, ((0, 8), (1, 4))),
        "lin_v": gaussian(arg_keys[2], (SEQUENCE_LENGTH, HEAD_COUNT * DH), 1.0, 6.0, ((0, 8), (1, 4))),
        "log_decay": draw_log_decay(jax.random.fold_in(arg_keys[7], 71), 0),
        "lin_gain": jnp.clip(1.0 + 0.18 * jax.random.normal(arg_keys[4], (HEAD_COUNT * DH,), jnp.float32), 0.1, 1.9),
        "soft_q": draw_soft_q(jax.random.fold_in(arg_keys[7], 71), 0),
        "soft_kv": draw_soft_kv(jax.random.fold_in(arg_keys[7], 71), 0),
    }


def rounded(x):
    return lax.optimization_barrier(x.astype(jnp.bfloat16)).astype(jnp.float32)

def block_terms(qb, kb, vb, gb, state):
    size = gb.shape[1]
    cum = jnp.cumsum(gb, axis=1)
    pos = jnp.arange(size)
    causal = pos[:, None] >= pos[None, :]
    diff = cum[:, :, None] - cum[:, None, :]
    weight = jnp.where(causal[None], jnp.exp(jnp.minimum(diff, 0.0)), 0.0)
    qf = qb.astype(jnp.float32)
    kf = kb.astype(jnp.float32)
    vf = vb.astype(jnp.float32)
    scores = jnp.einsum('thd,shd->hts', qf, kf)
    probs = rounded(scores * weight)
    intra = jnp.einsum('hts,shd->thd', probs, vf)
    inter = jnp.exp(cum).T[:, :, None] * jnp.einsum('thd,hde->the', qf, rounded(state))
    keys_scaled = rounded(kf * jnp.exp(cum[:, -1:] - cum).T[:, :, None])
    local = jnp.einsum('shd,she->hde', keys_scaled, vf)
    return (intra + inter, local, cum[:, -1])

def lightning_layer(lin_q, lin_k, lin_v, log_decay, lin_gain):
    nblk = SEQUENCE_LENGTH // BLOCK
    q = lin_q.reshape(nblk, BLOCK, HEAD_COUNT, DH)
    k = lin_k.reshape(nblk, BLOCK, HEAD_COUNT, DH)
    v = lin_v.reshape(nblk, BLOCK, HEAD_COUNT, DH)
    g = log_decay.reshape(HEAD_COUNT, nblk, BLOCK).transpose(1, 0, 2)

    def advance(state, xs):
        qb, kb, vb, gb = xs
        mixed, local, total = block_terms(qb, kb, vb, gb, state)
        state = jnp.exp(total)[:, None, None] * state + local
        return (state, mixed)
    init = jnp.zeros((HEAD_COUNT, DH, DH), jnp.float32)
    final, mixed = lax.scan(advance, init, (q, k, v, g))
    rms = jnp.sqrt(lax.optimization_barrier(jnp.mean(mixed * mixed, axis=-1, keepdims=True)) + 1e-05)
    normed = mixed / rms * lin_gain.reshape(HEAD_COUNT, DH)
    return normed.reshape(SEQUENCE_LENGTH, HEAD_COUNT * DH).astype(jnp.bfloat16)

def softmax_layer(soft_q, soft_kv):
    group = HEAD_COUNT // KVH
    q = soft_q.reshape(SEQUENCE_LENGTH, KVH, group, DH)
    kv = soft_kv.reshape(SEQUENCE_LENGTH, KVH, 2, DH)
    qblock = 256 if SEQUENCE_LENGTH % 256 == 0 else SEQUENCE_LENGTH
    nq = SEQUENCE_LENGTH // qblock
    scale = DH ** (-0.5)
    kpos = jnp.arange(SEQUENCE_LENGTH)

    def one_head(index):
        qn = lax.dynamic_index_in_dim(q, index, 1, keepdims=False).astype(jnp.float32)
        kvn = lax.dynamic_index_in_dim(kv, index, 1, keepdims=False).astype(jnp.float32)
        key_matrix = kvn[:, 0]
        value_rows = kvn[:, 1]

        def one_block(bidx):
            qblk = lax.dynamic_slice_in_dim(qn, bidx * qblock, qblock, 0)
            qpos = bidx * qblock + jnp.arange(qblock)
            scores = jnp.einsum('qgd,kd->gqk', qblk, key_matrix) * scale
            mask = kpos[None, :] <= qpos[:, None]
            scores = jnp.where(mask[None], scores, -jnp.inf)
            peak = lax.optimization_barrier(jnp.max(scores, axis=-1, keepdims=True))
            weights = jnp.where(mask[None], jnp.exp(scores - peak), 0.0)
            denom = lax.optimization_barrier(jnp.sum(weights, axis=-1))
            out = jnp.einsum('gqk,kd->gqd', rounded(weights), value_rows) / denom[:, :, None]
            return out.transpose(1, 0, 2)
        outs = lax.map(one_block, jnp.arange(nq))
        return outs.reshape(SEQUENCE_LENGTH, group, DH)
    heads = lax.map(one_head, jnp.arange(KVH))
    return heads.transpose(1, 0, 2, 3).reshape(SEQUENCE_LENGTH, HEAD_COUNT * DH).astype(jnp.bfloat16)

def reference(lin_q, lin_k, lin_v, log_decay, lin_gain, soft_q, soft_kv):
    lin_out = lightning_layer(lin_q, lin_k, lin_v, log_decay, lin_gain)
    soft_out = softmax_layer(soft_q, soft_kv)
    return (lin_out, soft_out)
```

```python
import functools
import math

import jax
import jax.numpy as jnp
from jax import lax
from jax.experimental import pallas as pl
from jax.experimental.pallas import tpu as pltpu
from jax.sharding import PartitionSpec as P

MESH = pl.DeviceIdType.MESH


def running_sum(x):
    size = x.shape[1]
    upper = jnp.triu(jnp.ones((size, size), x.dtype))
    return jnp.dot(x, upper, precision=lax.Precision.HIGHEST)


def block_local(kb, gb):
    cum = running_sum(gb)
    keys_scaled = (kb.astype(jnp.float32) * jnp.exp(cum[:, -1:] - cum).T[:, :, None]).astype(
        jnp.bfloat16
    )
    return (cum, keys_scaled)


def block_output(qb, kb, vb, cum, state):
    size = cum.shape[1]
    pos = jnp.arange(size)
    causal = pos[:, None] >= pos[None, :]
    diff = cum[:, :, None] - cum[:, None, :]
    weight = jnp.where(causal[None], jnp.exp(jnp.minimum(diff, 0.0)), 0.0)
    scores = jnp.einsum("thd,shd->hts", qb, kb, preferred_element_type=jnp.float32)
    probs = (scores * weight).astype(jnp.bfloat16)
    intra = jnp.einsum("hts,shd->thd", probs, vb, preferred_element_type=jnp.float32)
    inter = jnp.einsum(
        "thd,hde->the", qb, state.astype(jnp.bfloat16), preferred_element_type=jnp.float32
    )
    return intra + jnp.exp(cum).T[:, :, None] * inter


def join_states(earlier, later):
    return (later[0], jnp.exp(later[0])[:, None, None] * earlier[1] + later[1])


def lightning_part(lin_q, lin_k, lin_v, log_decay, lin_gain):
    tok, width = lin_q.shape
    heads = log_decay.shape[0]
    dim = width // heads
    q = lin_q.reshape(tok, heads, dim)
    k = lin_k.reshape(tok, heads, dim)
    v = lin_v.reshape(tok, heads, dim)
    total = (jnp.zeros((heads,), jnp.float32), jnp.zeros((heads, dim, dim), jnp.float32))
    cum, keys_scaled = block_local(k, log_decay)
    local = jnp.einsum("shd,she->hde", keys_scaled, v, preferred_element_type=jnp.float32)
    total = join_states(total, (cum[:, -1], local))
    logs = lax.all_gather(total[0][None], "ctx", axis=0, tiled=True)
    mine = lax.axis_index("ctx")
    csum = running_sum(logs.T).T
    before = jnp.sum(jnp.where((jnp.arange(logs.shape[0]) < mine)[:, None], logs, 0.0), axis=0)
    piece = lax.all_gather(total[1][None].astype(jnp.bfloat16), "ctx", axis=0, tiled=True).astype(
        jnp.float32
    )
    rows = piece.shape[0]
    idx = jnp.arange(rows)
    live = (idx < mine)[:, None]
    decay_factor = jnp.exp(jnp.where(live, before[None] - csum, -jnp.inf))
    state = jnp.zeros((heads, dim, dim), jnp.float32) + jnp.einsum(
        "jh,jhde->hde", decay_factor, piece, precision=lax.Precision.HIGHEST
    )
    mixed = block_output(q, k, v, cum, state)
    rms = jnp.sqrt(jnp.mean(mixed * mixed, axis=-1, keepdims=True) + 1e-05)
    outputs = mixed / rms * lin_gain.reshape(heads, dim)
    return outputs.reshape(tok, width).astype(jnp.bfloat16)


def softmax_part(soft_q, soft_kv, dim):
    local_q, local_kv = (
        lax.all_to_all(soft_q, "head", split_axis=1, concat_axis=0, tiled=True),
        lax.all_to_all(soft_kv, "head", split_axis=1, concat_axis=0, tiled=True),
    )
    tok = local_q.shape[0]
    half = tok // 2
    kvl = local_kv.shape[1] // (2 * dim)
    group = local_q.shape[1] // (dim * kvl)
    mine = lax.axis_index("ctx")
    first_q = local_q[:half]
    second_q = local_q[half:]
    second_start = mine * tok + half
    first_start = mine * tok
    first_pos = first_start + jnp.arange(half)
    second_pos = second_start + jnp.arange(half)
    first_heads = first_q.reshape(half, kvl, group, dim)
    second_heads = second_q.reshape(half, kvl, group, dim)
    scale = dim ** (-0.5)

    def update(carry, queries, qpos, kblock, kstart):
        peak, total, acc = carry
        size = kblock.shape[0]
        pair = kblock.reshape(size, kvl, 2, dim)
        key_matrix = pair[:, :, 0]
        value_rows = pair[:, :, 1]
        kpos = kstart + jnp.arange(size)
        mask = (kpos[None, :] <= qpos[:, None])[None, None]
        scores = (
            jnp.einsum("qngd,knd->ngqk", queries, key_matrix, preferred_element_type=jnp.float32)
            * scale
        )
        scores = jnp.where(mask, scores, -1e30)
        newpeak = jnp.maximum(peak, jnp.max(scores, axis=-1))
        weights = jnp.where(mask, jnp.exp(scores - newpeak[..., None]), 0.0)
        decay_factor = jnp.exp(peak - newpeak)
        total = total * decay_factor + jnp.sum(weights, axis=-1)
        acc = acc * decay_factor[..., None] + jnp.einsum(
            "ngqk,knd->ngqd",
            weights.astype(jnp.bfloat16),
            value_rows,
            preferred_element_type=jnp.float32,
        )
        return (newpeak, total, acc)

    def guarded(carry, queries, qpos, kblock, kstart):
        return update(carry, queries, qpos, kblock, kstart)

    def start_carry():
        return (
            jnp.full((kvl, group, half), -1e30, jnp.float32),
            jnp.zeros((kvl, group, half), jnp.float32),
            jnp.zeros((kvl, group, half, dim), jnp.float32),
        )

    def finish(carry):
        peak, total, acc = carry
        result = acc / total[..., None]
        return result.transpose(2, 0, 1, 3).reshape(half, kvl * group * dim).astype(jnp.bfloat16)

    piece = lax.all_gather(local_kv, "ctx", axis=0, tiled=True)
    rows = piece.shape[0]
    width = math.gcd(rows, 512)

    def step(index, inner):
        kblock = lax.dynamic_slice_in_dim(piece, index * width, width, 0)
        kstart = index * width
        early = guarded(inner[0], first_heads, first_pos, kblock, kstart)
        later = guarded(inner[1], second_heads, second_pos, kblock, kstart)
        return (early, later)

    early, later = lax.fori_loop(0, rows // width, step, (start_carry(), start_carry()))
    first_out = finish(early)
    second_out = finish(later)
    result = jnp.concatenate([first_out, second_out], axis=0)
    return lax.all_to_all(result, "head", split_axis=0, concat_axis=1, tiled=True)


def mixer_kernel(
    nctx, nz, dim,
    lq, lk, lv, ld, gain, sq, skv,
    lin_out, soft_out,
    kv_all, q_all, st_send, st_recv, tot_send, tot_recv, pre_send, state_in, cum, mix, out_send,
    own_sem, kv_ss, kv_rs, q_ss, q_rs, z_ss, z_rs, st_ss, st_rs, tt_ss, tt_rs, pr_ss, pr_rs,
    o_ss, o_rs,
):
    me = lax.axis_index("ctx")
    zme = lax.axis_index("head")
    tok = lq.shape[0]
    heads = ld.shape[0]
    rows = sq.shape[0]
    qw = sq.shape[1] // nctx
    group = qw // dim
    hpo = heads // nctx
    f32, bf16 = jnp.float32, jnp.bfloat16

    def ctx_peer(k):
        return lax.rem(me + k, nctx)

    def z_peer(k):
        return lax.rem(zme + k, nz)

    barrier = pltpu.get_barrier_semaphore()
    for k in range(1, nctx):
        pl.semaphore_signal(barrier, inc=1, device_id=(ctx_peer(k), zme), device_id_type=MESH)
    for k in range(1, nz):
        pl.semaphore_signal(barrier, inc=1, device_id=(me, z_peer(k)), device_id_type=MESH)
    pl.semaphore_wait(barrier, nctx + nz - 2)

    def remote(src, dst, ss, rs, k, device):
        return pltpu.make_async_remote_copy(
            src_ref=src, dst_ref=dst, send_sem=ss.at[k], recv_sem=rs.at[k],
            device_id=device, device_id_type=MESH,
        )

    def cols(index, width):
        return pl.ds(pl.multiple_of(index * width, width), width)

    def kv_copy(k):
        d = ctx_peer(k)
        return remote(skv.at[:, cols(d, 2 * dim)], kv_all.at[zme, me], kv_ss, kv_rs, k, (d, zme))

    def q_copy(k):
        d = ctx_peer(k)
        return remote(sq.at[:, cols(d, qw)], q_all.at[me], q_ss, q_rs, k, (d, zme))

    def z_copy(k):
        return remote(kv_all.at[zme], kv_all.at[zme], z_ss, z_rs, k, (me, z_peer(k)))

    def st_copy(k):
        d = ctx_peer(k)
        return remote(st_send.at[d], st_recv.at[me], st_ss, st_rs, k, (d, zme))

    def tt_copy(k):
        d = ctx_peer(k)
        return remote(tot_send.at[d], tot_recv.at[me], tt_ss, tt_rs, k, (d, zme))

    def pre_copy(k):
        d = ctx_peer(k)
        return remote(pre_send.at[d], state_in.at[me], pr_ss, pr_rs, k, (d, zme))

    def out_copy(d, k):
        return remote(out_send.at[d], soft_out.at[:, cols(me, qw)], o_ss, o_rs, k, (d, zme))

    own_kv = pltpu.make_async_copy(skv.at[:, cols(me, 2 * dim)], kv_all.at[zme, me], own_sem.at[0])
    own_q = pltpu.make_async_copy(sq.at[:, cols(me, qw)], q_all.at[me], own_sem.at[1])
    own_out = pltpu.make_async_copy(
        out_send.at[me], soft_out.at[:, cols(me, qw)], own_sem.at[2]
    )
    own_kv.start()
    for k in range(1, nctx):
        kv_copy(k).start()
    own_q.start()
    for k in range(1, nctx):
        q_copy(k).start()

    low = lax.broadcasted_iota(jnp.int32, (tok, tok), 1) <= lax.broadcasted_iota(
        jnp.int32, (tok, tok), 0
    )
    tri = jnp.where(low, 1.0, 0.0).astype(bf16)

    def running(part, wide):
        return lax.dot_general(tri, part, (((1,), (1,)), ((), ())), preferred_element_type=f32)

    def local_state(j, carry):
        for r in range(hpo):
            h = j * hpo + r
            g = jnp.broadcast_to(ld[pl.ds(h, 1), :], (dim, tok))
            g0 = g.astype(bf16)
            rest = g - g0.astype(f32)
            g1 = rest.astype(bf16)
            g2 = (rest - g1.astype(f32)).astype(bf16)
            c = running(g0, dim) + running(g1, dim) + running(g2, dim)
            cum[h] = c
            last = c[tok - 1 : tok, :]
            tot_send[j, pl.ds(r, 1), :] = last
            ks = (lk[:, cols(h, dim)].astype(f32) * jnp.exp(last - c)).astype(bf16)
            st_send[j, r] = lax.dot_general(
                ks, lv[:, cols(h, dim)], (((0,), (0,)), ((), ())), preferred_element_type=f32
            ).astype(bf16)
        return carry

    tot_send[...] = jnp.zeros_like(tot_send)
    lax.fori_loop(0, nctx, local_state, 0)

    own_kv.wait()
    for k in range(1, nctx):
        kv_copy(k).wait_recv()
    for k in range(1, nz):
        z_copy(k).start()
    for k in range(1, nctx):
        st_copy(k).start()
        tt_copy(k).start()
    st_recv[me] = st_send[me]
    tot_recv[me] = tot_send[me]

    def intra(h, carry):
        c = cum[h]
        wide = jnp.concatenate([c] * (tok // dim), axis=1)
        row = jnp.transpose(c)[0:1, :]
        weight = jnp.where(low, jnp.exp(jnp.minimum(wide - row, 0.0)), 0.0)
        s = lax.dot_general(
            lq[:, cols(h, dim)], lk[:, cols(h, dim)], (((1,), (1,)), ((), ())),
            preferred_element_type=f32,
        )
        probs = (s * weight).astype(bf16)
        mix[h] = jnp.dot(probs, lv[:, cols(h, dim)], preferred_element_type=f32)
        return carry

    lax.fori_loop(0, heads, intra, 0)

    for k in range(1, nctx):
        st_copy(k).wait_recv()
        tt_copy(k).wait_recv()
    state = [jnp.zeros((dim, dim), f32) for _ in range(hpo)]
    for c in range(nctx):
        for r in range(hpo):
            pre_send[c, r] = state[r].astype(bf16)
            decay = jnp.exp(tot_recv[c, r : r + 1, :])
            state[r] = decay * state[r] + st_recv[c, r].astype(f32)
    for k in range(1, nctx):
        pre_copy(k).start()
    state_in[me] = pre_send[me]

    own_q.wait()
    for k in range(1, nctx):
        q_copy(k).wait_recv()
    for k in range(1, nz):
        z_copy(k).wait_recv()
    factor = dim ** (-0.5) * math.log2(math.e)
    per = max(1, min(group, tok // rows))
    for c in range(nctx):
        for t in range(group // per):
            q = jnp.concatenate(
                [
                    q_all[c, :, (t * per + i) * dim : (t * per + i + 1) * dim]
                    for i in range(per)
                ],
                axis=0,
            )
            kd = kv_all[:, c, :, :dim].reshape(nz * rows, dim)
            vd = kv_all[:, c, :, dim:].reshape(nz * rows, dim)
            sd = lax.dot_general(q, kd, (((1,), (1,)), ((), ())), preferred_element_type=f32)
            kpos = lax.broadcasted_iota(jnp.int32, sd.shape, 1)
            qpos = zme * rows + lax.rem(lax.broadcasted_iota(jnp.int32, sd.shape, 0), rows)
            sd = jnp.where(kpos <= qpos, sd, -1e30)
            peak = jnp.max(sd, axis=1, keepdims=True)
            if c > 0:
                kp = kv_all[:, :c, :, :dim].reshape(nz * c * rows, dim)
                vp = kv_all[:, :c, :, dim:].reshape(nz * c * rows, dim)
                sp = lax.dot_general(q, kp, (((1,), (1,)), ((), ())), preferred_element_type=f32)
                peak = jnp.maximum(peak, jnp.max(sp, axis=1, keepdims=True))
            wd = jnp.exp2((sd - peak) * factor)
            total = jnp.sum(wd, axis=1, keepdims=True)
            acc = jnp.dot(wd.astype(bf16), vd, preferred_element_type=f32)
            if c > 0:
                wp = jnp.exp2((sp - peak) * factor)
                total = total + jnp.sum(wp, axis=1, keepdims=True)
                acc = acc + jnp.dot(wp.astype(bf16), vp, preferred_element_type=f32)
            out = (acc / total).astype(bf16)
            for i in range(per):
                out_send[c, :, (t * per + i) * dim : (t * per + i + 1) * dim] = out[
                    i * rows : (i + 1) * rows
                ]

        @pl.when(me == c)
        def _():
            own_out.start()

        @pl.when(me != c)
        def _():
            out_copy(c, lax.rem(c - me + nctx, nctx)).start()

    for k in range(1, nctx):
        pre_copy(k).wait_recv()

    def finish(j, carry):
        for r in range(hpo):
            h = j * hpo + r
            inter = jnp.dot(lq[:, cols(h, dim)], state_in[j, r], preferred_element_type=f32)
            m = mix[h] + jnp.exp(cum[h]) * inter
            ms = jnp.mean(m * m, axis=1, keepdims=True)
            lin_out[:, cols(h, dim)] = (
                m * lax.rsqrt(ms + 1e-05) * gain[:, cols(h, dim)]
            ).astype(bf16)
        return carry

    lax.fori_loop(0, nctx, finish, 0)

    own_out.wait()
    for k in range(1, nctx):
        out_copy(ctx_peer(k), k).wait()
        kv_copy(k).wait_send()
        q_copy(k).wait_send()
        st_copy(k).wait_send()
        tt_copy(k).wait_send()
        pre_copy(k).wait_send()
    for k in range(1, nz):
        z_copy(k).wait_send()


def fused_body(nctx, nz, lin_q, lin_k, lin_v, log_decay, lin_gain, soft_q, soft_kv):
    tok, width = lin_q.shape
    heads = log_decay.shape[0]
    dim = width // heads
    rows = soft_q.shape[0]
    qw = soft_q.shape[1] // nctx
    hpo = heads // nctx
    f32, bf16 = jnp.float32, jnp.bfloat16
    vmem = pl.BlockSpec(memory_space=pltpu.VMEM)
    hbm = pl.BlockSpec(memory_space=pl.ANY)
    dma = pltpu.SemaphoreType.DMA
    return pl.pallas_call(
        functools.partial(mixer_kernel, nctx, nz, dim),
        out_shape=(
            jax.ShapeDtypeStruct(lin_q.shape, bf16),
            jax.ShapeDtypeStruct(soft_q.shape, bf16),
        ),
        in_specs=[vmem] * 5 + [hbm] * 2,
        out_specs=(vmem, hbm),
        scratch_shapes=[
            pltpu.VMEM((nz, nctx, rows, 2 * dim), bf16),
            pltpu.VMEM((nctx, rows, qw), bf16),
            pltpu.VMEM((nctx, hpo, dim, dim), bf16),
            pltpu.VMEM((nctx, hpo, dim, dim), bf16),
            pltpu.VMEM((nctx, 8, dim), f32),
            pltpu.VMEM((nctx, 8, dim), f32),
            pltpu.VMEM((nctx, hpo, dim, dim), bf16),
            pltpu.VMEM((nctx, hpo, dim, dim), bf16),
            pltpu.VMEM((heads, tok, dim), f32),
            pltpu.VMEM((heads, tok, dim), f32),
            pltpu.VMEM((nctx, rows, qw), bf16),
            dma((3,)),
            dma((nctx,)), dma((nctx,)),
            dma((nctx,)), dma((nctx,)),
            dma((nz,)), dma((nz,)),
            dma((nctx,)), dma((nctx,)),
            dma((nctx,)), dma((nctx,)),
            dma((nctx,)), dma((nctx,)),
            dma((nctx,)), dma((nctx,)),
        ],
        compiler_params=pltpu.CompilerParams(
            collective_id=0, has_side_effects=True, vmem_limit_bytes=50 * 1024 * 1024
        ),
        cost_estimate=pl.CostEstimate(
            flops=4 * 10**9, bytes_accessed=8 * 10**6, transcendentals=6 * 10**6
        ),
        name="mixers",
    )(lin_q, lin_k, lin_v, log_decay, lin_gain.reshape(1, width), soft_q, soft_kv)


def body(nctx, nz, lin_q, lin_k, lin_v, log_decay, lin_gain, soft_q, soft_kv):
    heads = log_decay.shape[0]
    dim = lin_q.shape[1] // heads
    kv_heads = soft_kv.shape[1] // (2 * dim)
    if kv_heads == nctx and heads % nctx == 0 and heads // nctx <= 8:
        return fused_body(
            nctx, nz, lin_q, lin_k, lin_v, log_decay, lin_gain, soft_q, soft_kv
        )
    lin_out = lightning_part(lin_q, lin_k, lin_v, log_decay, lin_gain)
    soft_out = softmax_part(soft_q, soft_kv, dim)
    return (lin_out, soft_out)


def solution(mesh):
    return jax.shard_map(
        functools.partial(body, mesh.shape["ctx"], mesh.shape["head"]),
        mesh=mesh,
        in_specs=(
            P("ctx", "head"),
            P("ctx", "head"),
            P("ctx", "head"),
            P("head", "ctx"),
            P("head"),
            P(("ctx", "head"), None),
            P(("ctx", "head"), None),
        ),
        out_specs=(P("ctx", "head"), P(("ctx", "head"), None)),
        check_vma=False,
    )
```

```python
import functools
import math

import jax
import jax.numpy as jnp
from jax import lax
from jax.experimental import pallas as pl
from jax.experimental.pallas import tpu as pltpu
from jax.sharding import PartitionSpec as P

MESH = pl.DeviceIdType.MESH


def running_sum(x):
    size = x.shape[1]
    upper = jnp.triu(jnp.ones((size, size), x.dtype))
    return jnp.dot(x, upper, precision=lax.Precision.HIGHEST)


def block_local(kb, gb):
    cum = running_sum(gb)
    keys_scaled = (kb.astype(jnp.float32) * jnp.exp(cum[:, -1:] - cum).T[:, :, None]).astype(
        jnp.bfloat16
    )
    return (cum, keys_scaled)


def block_output(qb, kb, vb, cum, state):
    size = cum.shape[1]
    pos = jnp.arange(size)
    causal = pos[:, None] >= pos[None, :]
    diff = cum[:, :, None] - cum[:, None, :]
    weight = jnp.where(causal[None], jnp.exp(jnp.minimum(diff, 0.0)), 0.0)
    scores = jnp.einsum("thd,shd->hts", qb, kb, preferred_element_type=jnp.float32)
    probs = (scores * weight).astype(jnp.bfloat16)
    intra = jnp.einsum("hts,shd->thd", probs, vb, preferred_element_type=jnp.float32)
    inter = jnp.einsum(
        "thd,hde->the", qb, state.astype(jnp.bfloat16), preferred_element_type=jnp.float32
    )
    return intra + jnp.exp(cum).T[:, :, None] * inter


def join_states(earlier, later):
    return (later[0], jnp.exp(later[0])[:, None, None] * earlier[1] + later[1])


def lightning_part(lin_q, lin_k, lin_v, log_decay, lin_gain):
    tok, width = lin_q.shape
    heads = log_decay.shape[0]
    dim = width // heads
    q = lin_q.reshape(tok, heads, dim)
    k = lin_k.reshape(tok, heads, dim)
    v = lin_v.reshape(tok, heads, dim)
    total = (jnp.zeros((heads,), jnp.float32), jnp.zeros((heads, dim, dim), jnp.float32))
    cum, keys_scaled = block_local(k, log_decay)
    local = jnp.einsum("shd,she->hde", keys_scaled, v, preferred_element_type=jnp.float32)
    total = join_states(total, (cum[:, -1], local))
    logs = lax.all_gather(total[0][None], "ctx", axis=0, tiled=True)
    mine = lax.axis_index("ctx")
    csum = running_sum(logs.T).T
    before = jnp.sum(jnp.where((jnp.arange(logs.shape[0]) < mine)[:, None], logs, 0.0), axis=0)
    piece = lax.all_gather(total[1][None].astype(jnp.bfloat16), "ctx", axis=0, tiled=True).astype(
        jnp.float32
    )
    rows = piece.shape[0]
    idx = jnp.arange(rows)
    live = (idx < mine)[:, None]
    decay_factor = jnp.exp(jnp.where(live, before[None] - csum, -jnp.inf))
    state = jnp.zeros((heads, dim, dim), jnp.float32) + jnp.einsum(
        "jh,jhde->hde", decay_factor, piece, precision=lax.Precision.HIGHEST
    )
    mixed = block_output(q, k, v, cum, state)
    rms = jnp.sqrt(jnp.mean(mixed * mixed, axis=-1, keepdims=True) + 1e-05)
    outputs = mixed / rms * lin_gain.reshape(heads, dim)
    return outputs.reshape(tok, width).astype(jnp.bfloat16)


def softmax_part(soft_q, soft_kv, dim):
    local_q, local_kv = (
        lax.all_to_all(soft_q, "head", split_axis=1, concat_axis=0, tiled=True),
        lax.all_to_all(soft_kv, "head", split_axis=1, concat_axis=0, tiled=True),
    )
    tok = local_q.shape[0]
    half = tok // 2
    kvl = local_kv.shape[1] // (2 * dim)
    group = local_q.shape[1] // (dim * kvl)
    mine = lax.axis_index("ctx")
    first_q = local_q[:half]
    second_q = local_q[half:]
    second_start = mine * tok + half
    first_start = mine * tok
    first_pos = first_start + jnp.arange(half)
    second_pos = second_start + jnp.arange(half)
    first_heads = first_q.reshape(half, kvl, group, dim)
    second_heads = second_q.reshape(half, kvl, group, dim)
    scale = dim ** (-0.5)

    def update(carry, queries, qpos, kblock, kstart):
        peak, total, acc = carry
        size = kblock.shape[0]
        pair = kblock.reshape(size, kvl, 2, dim)
        key_matrix = pair[:, :, 0]
        value_rows = pair[:, :, 1]
        kpos = kstart + jnp.arange(size)
        mask = (kpos[None, :] <= qpos[:, None])[None, None]
        scores = (
            jnp.einsum("qngd,knd->ngqk", queries, key_matrix, preferred_element_type=jnp.float32)
            * scale
        )
        scores = jnp.where(mask, scores, -1e30)
        newpeak = jnp.maximum(peak, jnp.max(scores, axis=-1))
        weights = jnp.where(mask, jnp.exp(scores - newpeak[..., None]), 0.0)
        decay_factor = jnp.exp(peak - newpeak)
        total = total * decay_factor + jnp.sum(weights, axis=-1)
        acc = acc * decay_factor[..., None] + jnp.einsum(
            "ngqk,knd->ngqd",
            weights.astype(jnp.bfloat16),
            value_rows,
            preferred_element_type=jnp.float32,
        )
        return (newpeak, total, acc)

    def guarded(carry, queries, qpos, kblock, kstart):
        return update(carry, queries, qpos, kblock, kstart)

    def start_carry():
        return (
            jnp.full((kvl, group, half), -1e30, jnp.float32),
            jnp.zeros((kvl, group, half), jnp.float32),
            jnp.zeros((kvl, group, half, dim), jnp.float32),
        )

    def finish(carry):
        peak, total, acc = carry
        result = acc / total[..., None]
        return result.transpose(2, 0, 1, 3).reshape(half, kvl * group * dim).astype(jnp.bfloat16)

    piece = lax.all_gather(local_kv, "ctx", axis=0, tiled=True)
    rows = piece.shape[0]
    width = math.gcd(rows, 512)

    def step(index, inner):
        kblock = lax.dynamic_slice_in_dim(piece, index * width, width, 0)
        kstart = index * width
        early = guarded(inner[0], first_heads, first_pos, kblock, kstart)
        later = guarded(inner[1], second_heads, second_pos, kblock, kstart)
        return (early, later)

    early, later = lax.fori_loop(0, rows // width, step, (start_carry(), start_carry()))
    first_out = finish(early)
    second_out = finish(later)
    result = jnp.concatenate([first_out, second_out], axis=0)
    return lax.all_to_all(result, "head", split_axis=0, concat_axis=1, tiled=True)


def mixer_kernel(
    nctx, nz, dim,
    lq_in, lk_in, lv_in, ld_in, gain_in, sq, skv,
    lin_out, soft_out,
    kv_all, q_all, st_send, st_recv, tot_send, tot_recv, pre_send, state_in, cum, mix, out_send,
    lq, lk, lv, ld, gain, in_sem, own_sem, kv_ss, kv_rs, q_ss, q_rs, z_ss, z_rs, st_ss, st_rs, tt_ss, tt_rs, pr_ss, pr_rs,
    o_ss, o_rs,
):
    me = lax.axis_index("ctx")
    zme = lax.axis_index("head")
    tok = lq.shape[0]
    heads = ld.shape[0]
    rows = sq.shape[0]
    qw = sq.shape[1] // nctx
    group = qw // dim
    hpo = heads // nctx
    f32, bf16 = jnp.float32, jnp.bfloat16

    def ctx_peer(k):
        return lax.rem(me + k, nctx)

    def z_peer(k):
        return lax.rem(zme + k, nz)

    loads = [
        pltpu.make_async_copy(src, dst, in_sem.at[i])
        for i, (src, dst) in enumerate(
            [(ld_in, ld), (lk_in, lk), (lv_in, lv), (lq_in, lq), (gain_in, gain)]
        )
    ]
    barrier = pltpu.get_barrier_semaphore()
    for k in range(1, nctx):
        pl.semaphore_signal(barrier, inc=1, device_id=(ctx_peer(k), zme), device_id_type=MESH)
    for k in range(1, nz):
        pl.semaphore_signal(barrier, inc=1, device_id=(me, z_peer(k)), device_id_type=MESH)
    for load in loads:
        load.start()
    pl.semaphore_wait(barrier, nctx + nz - 2)

    def remote(src, dst, ss, rs, k, device):
        return pltpu.make_async_remote_copy(
            src_ref=src, dst_ref=dst, send_sem=ss.at[k], recv_sem=rs.at[k],
            device_id=device, device_id_type=MESH,
        )

    def cols(index, width):
        return pl.ds(pl.multiple_of(index * width, width), width)

    def kv_copy(k):
        d = ctx_peer(k)
        return remote(skv.at[:, cols(d, 2 * dim)], kv_all.at[zme, me], kv_ss, kv_rs, k, (d, zme))

    def q_copy(k):
        d = ctx_peer(k)
        return remote(sq.at[:, cols(d, qw)], q_all.at[me], q_ss, q_rs, k, (d, zme))

    def z_copy(src, step):
        to = jnp.clip(zme + step, 0, nz - 1)
        slot = src if step > 0 else nz + src
        return pltpu.make_async_remote_copy(
            src_ref=kv_all.at[src], dst_ref=kv_all.at[src], send_sem=z_ss.at[slot],
            recv_sem=z_rs.at[src], device_id=(me, to), device_id_type=MESH,
        )

    def z_relay(away):
        @pl.when(zme >= away)
        def _():
            if away > 0:
                z_copy(zme - away, 1).wait_recv()

            @pl.when(zme < nz - 1)
            def _():
                z_copy(zme - away, 1).start()

        @pl.when(zme < nz - away)
        def _():
            if away > 0:
                z_copy(zme + away, -1).wait_recv()

            @pl.when(zme > 0)
            def _():
                z_copy(zme + away, -1).start()

    def st_copy(k):
        d = ctx_peer(k)
        return remote(st_send.at[d], st_recv.at[me], st_ss, st_rs, k, (d, zme))

    def tt_copy(k):
        d = ctx_peer(k)
        return remote(tot_send.at[d], tot_recv.at[me], tt_ss, tt_rs, k, (d, zme))

    def pre_copy(k):
        d = ctx_peer(k)
        return remote(pre_send.at[d], state_in.at[me], pr_ss, pr_rs, k, (d, zme))

    def out_copy(d, k):
        return remote(out_send.at[d], soft_out.at[:, cols(me, qw)], o_ss, o_rs, k, (d, zme))

    own_kv = pltpu.make_async_copy(skv.at[:, cols(me, 2 * dim)], kv_all.at[zme, me], own_sem.at[0])
    own_q = pltpu.make_async_copy(sq.at[:, cols(me, qw)], q_all.at[me], own_sem.at[1])
    own_out = pltpu.make_async_copy(
        out_send.at[me], soft_out.at[:, cols(me, qw)], own_sem.at[2]
    )
    own_kv.start()
    for k in range(1, nctx):
        kv_copy(k).start()
    own_q.start()
    for k in range(1, nctx):
        q_copy(k).start()

    low = lax.broadcasted_iota(jnp.int32, (tok, tok), 1) <= lax.broadcasted_iota(
        jnp.int32, (tok, tok), 0
    )
    tri = jnp.where(low, 1.0, 0.0).astype(bf16)

    def running(part, wide):
        return lax.dot_general(tri, part, (((1,), (1,)), ((), ())), preferred_element_type=f32)

    def local_state(j, carry):
        for r in range(hpo):
            h = j * hpo + r
            g = jnp.broadcast_to(ld[pl.ds(h, 1), :], (dim, tok))
            g0 = g.astype(bf16)
            rest = g - g0.astype(f32)
            g1 = rest.astype(bf16)
            g2 = (rest - g1.astype(f32)).astype(bf16)
            c = running(g0, dim) + running(g1, dim) + running(g2, dim)
            cum[h] = c
            last = c[tok - 1 : tok, :]
            tot_send[j, pl.ds(r, 1), :] = last
            ks = (lk[:, cols(h, dim)].astype(f32) * jnp.exp(last - c)).astype(bf16)
            st_send[j, r] = lax.dot_general(
                ks, lv[:, cols(h, dim)], (((0,), (0,)), ((), ())), preferred_element_type=f32
            ).astype(bf16)
        return carry

    tot_send[...] = jnp.zeros_like(tot_send)
    for load in loads:
        load.wait()
    lax.fori_loop(0, nctx, local_state, 0)

    own_kv.wait()
    for k in range(1, nctx):
        kv_copy(k).wait_recv()
    z_relay(0)
    for k in range(1, nctx):
        st_copy(k).start()
        tt_copy(k).start()
    st_recv[me] = st_send[me]
    tot_recv[me] = tot_send[me]

    def intra(h, carry):
        c = cum[h]
        wide = jnp.concatenate([c] * (tok // dim), axis=1)
        row = jnp.transpose(c)[0:1, :]
        weight = jnp.where(low, jnp.exp(jnp.minimum(wide - row, 0.0)), 0.0)
        s = lax.dot_general(
            lq[:, cols(h, dim)], lk[:, cols(h, dim)], (((1,), (1,)), ((), ())),
            preferred_element_type=f32,
        )
        probs = (s * weight).astype(bf16)
        mix[h] = jnp.dot(probs, lv[:, cols(h, dim)], preferred_element_type=f32)
        return carry

    for part in range(1, nz):
        lax.fori_loop(heads * (part - 1) // (nz - 1), heads * part // (nz - 1), intra, 0)
        if part < nz - 1:
            z_relay(part)

    for k in range(1, nctx):
        st_copy(k).wait_recv()
        tt_copy(k).wait_recv()
    state = [jnp.zeros((dim, dim), f32) for _ in range(hpo)]
    for c in range(nctx):
        for r in range(hpo):
            pre_send[c, r] = state[r].astype(bf16)
            decay = jnp.exp(tot_recv[c, r : r + 1, :])
            state[r] = decay * state[r] + st_recv[c, r].astype(f32)
    for k in range(1, nctx):
        pre_copy(k).start()
    state_in[me] = pre_send[me]

    own_q.wait()
    for k in range(1, nctx):
        q_copy(k).wait_recv()
    z_relay(nz - 1)
    factor = dim ** (-0.5) * math.log2(math.e)
    per = max(1, min(group, tok // rows))
    def attend(c):
        for t in range(group // per):
            q = jnp.concatenate(
                [
                    q_all[c, :, (t * per + i) * dim : (t * per + i + 1) * dim]
                    for i in range(per)
                ],
                axis=0,
            )
            kd = kv_all[:, c, :, :dim].reshape(nz * rows, dim)
            vd = kv_all[:, c, :, dim:].reshape(nz * rows, dim)
            sd = lax.dot_general(q, kd, (((1,), (1,)), ((), ())), preferred_element_type=f32)
            kpos = lax.broadcasted_iota(jnp.int32, sd.shape, 1)
            qpos = zme * rows + lax.rem(lax.broadcasted_iota(jnp.int32, sd.shape, 0), rows)
            sd = jnp.where(kpos <= qpos, sd, -1e30)
            peak = jnp.max(sd, axis=1, keepdims=True)
            if c > 0:
                kp = kv_all[:, :c, :, :dim].reshape(nz * c * rows, dim)
                vp = kv_all[:, :c, :, dim:].reshape(nz * c * rows, dim)
                sp = lax.dot_general(q, kp, (((1,), (1,)), ((), ())), preferred_element_type=f32)
                peak = jnp.maximum(peak, jnp.max(sp, axis=1, keepdims=True))
            wd = jnp.exp2((sd - peak) * factor)
            total = jnp.sum(wd, axis=1, keepdims=True)
            acc = jnp.dot(wd.astype(bf16), vd, preferred_element_type=f32)
            if c > 0:
                wp = jnp.exp2((sp - peak) * factor)
                total = total + jnp.sum(wp, axis=1, keepdims=True)
                acc = acc + jnp.dot(wp.astype(bf16), vp, preferred_element_type=f32)
            out = (acc / total).astype(bf16)
            for i in range(per):
                out_send[c, :, (t * per + i) * dim : (t * per + i + 1) * dim] = out[
                    i * rows : (i + 1) * rows
                ]

    def turn(k, carry):
        c = ctx_peer(k)
        lax.switch(c, [functools.partial(attend, i) for i in range(nctx)])

        @pl.when(k == nctx)
        def _():
            own_out.start()

        @pl.when(k < nctx)
        def _():
            out_copy(c, k).start()

        return carry

    lax.fori_loop(1, nctx + 1, turn, 0)

    for k in range(1, nctx):
        pre_copy(k).wait_recv()

    def finish(j, carry):
        for r in range(hpo):
            h = j * hpo + r
            inter = jnp.dot(lq[:, cols(h, dim)], state_in[j, r], preferred_element_type=f32)
            m = mix[h] + jnp.exp(cum[h]) * inter
            ms = jnp.mean(m * m, axis=1, keepdims=True)
            lin_out[:, cols(h, dim)] = (
                m * lax.rsqrt(ms + 1e-05) * gain[:, cols(h, dim)]
            ).astype(bf16)
        return carry

    lax.fori_loop(0, nctx, finish, 0)

    own_out.wait()
    for k in range(1, nctx):
        out_copy(ctx_peer(k), k).wait()
        kv_copy(k).wait_send()
        q_copy(k).wait_send()
        st_copy(k).wait_send()
        tt_copy(k).wait_send()
        pre_copy(k).wait_send()
    for away in range(nz):

        @pl.when((zme >= away) & (zme < nz - 1))
        def _(away=away):
            z_copy(zme - away, 1).wait_send()

        @pl.when((zme < nz - away) & (zme > 0))
        def _(away=away):
            z_copy(zme + away, -1).wait_send()


def fused_body(nctx, nz, lin_q, lin_k, lin_v, log_decay, lin_gain, soft_q, soft_kv):
    tok, width = lin_q.shape
    heads = log_decay.shape[0]
    dim = width // heads
    rows = soft_q.shape[0]
    qw = soft_q.shape[1] // nctx
    hpo = heads // nctx
    f32, bf16 = jnp.float32, jnp.bfloat16
    vmem = pl.BlockSpec(memory_space=pltpu.VMEM)
    hbm = pl.BlockSpec(memory_space=pltpu.HBM)
    anywhere = pl.BlockSpec(memory_space=pl.ANY)
    dma = pltpu.SemaphoreType.DMA
    return pl.pallas_call(
        functools.partial(mixer_kernel, nctx, nz, dim),
        out_shape=(
            jax.ShapeDtypeStruct(lin_q.shape, bf16),
            jax.ShapeDtypeStruct(soft_q.shape, bf16),
        ),
        in_specs=[hbm] * 7,
        out_specs=(vmem, anywhere),
        scratch_shapes=[
            pltpu.VMEM((nz, nctx, rows, 2 * dim), bf16),
            pltpu.VMEM((nctx, rows, qw), bf16),
            pltpu.VMEM((nctx, hpo, dim, dim), bf16),
            pltpu.VMEM((nctx, hpo, dim, dim), bf16),
            pltpu.VMEM((nctx, 8, dim), f32),
            pltpu.VMEM((nctx, 8, dim), f32),
            pltpu.VMEM((nctx, hpo, dim, dim), bf16),
            pltpu.VMEM((nctx, hpo, dim, dim), bf16),
            pltpu.VMEM((heads, tok, dim), f32),
            pltpu.VMEM((heads, tok, dim), f32),
            pltpu.VMEM((nctx, rows, qw), bf16),
            pltpu.VMEM(lin_q.shape, bf16),
            pltpu.VMEM(lin_q.shape, bf16),
            pltpu.VMEM(lin_q.shape, bf16),
            pltpu.VMEM(log_decay.shape, f32),
            pltpu.VMEM((1, width), f32),
            dma((5,)),
            dma((3,)),
            dma((nctx,)), dma((nctx,)),
            dma((nctx,)), dma((nctx,)),
            dma((2 * nz,)), dma((nz,)),
            dma((nctx,)), dma((nctx,)),
            dma((nctx,)), dma((nctx,)),
            dma((nctx,)), dma((nctx,)),
            dma((nctx,)), dma((nctx,)),
        ],
        compiler_params=pltpu.CompilerParams(
            collective_id=0, has_side_effects=True, vmem_limit_bytes=50 * 1024 * 1024
        ),
        cost_estimate=pl.CostEstimate(
            flops=4 * 10**9, bytes_accessed=8 * 10**6, transcendentals=6 * 10**6
        ),
        name="mixers",
    )(lin_q, lin_k, lin_v, log_decay, lin_gain.reshape(1, width), soft_q, soft_kv)


def body(nctx, nz, lin_q, lin_k, lin_v, log_decay, lin_gain, soft_q, soft_kv):
    heads = log_decay.shape[0]
    dim = lin_q.shape[1] // heads
    kv_heads = soft_kv.shape[1] // (2 * dim)
    if kv_heads == nctx and heads % nctx == 0 and heads // nctx <= 8:
        return fused_body(
            nctx, nz, lin_q, lin_k, lin_v, log_decay, lin_gain, soft_q, soft_kv
        )
    lin_out = lightning_part(lin_q, lin_k, lin_v, log_decay, lin_gain)
    soft_out = softmax_part(soft_q, soft_kv, dim)
    return (lin_out, soft_out)


def solution(mesh):
    return jax.shard_map(
        functools.partial(body, mesh.shape["ctx"], mesh.shape["head"]),
        mesh=mesh,
        in_specs=(
            P("ctx", "head"),
            P("ctx", "head"),
            P("ctx", "head"),
            P("head", "ctx"),
            P("head"),
            P(("ctx", "head"), None),
            P(("ctx", "head"), None),
        ),
        out_specs=(P("ctx", "head"), P(("ctx", "head"), None)),
        check_vma=False,
    )
```

```python
import functools
import math

import jax
import jax.numpy as jnp
from jax import lax
from jax.experimental import pallas as pl
from jax.experimental.pallas import tpu as pltpu
from jax.sharding import PartitionSpec as P

MESH = pl.DeviceIdType.MESH


def running_sum(x):
    size = x.shape[1]
    upper = jnp.triu(jnp.ones((size, size), x.dtype))
    return jnp.dot(x, upper, precision=lax.Precision.HIGHEST)


def block_local(kb, gb):
    cum = running_sum(gb)
    keys_scaled = (kb.astype(jnp.float32) * jnp.exp(cum[:, -1:] - cum).T[:, :, None]).astype(
        jnp.bfloat16
    )
    return (cum, keys_scaled)


def block_output(qb, kb, vb, cum, state):
    size = cum.shape[1]
    pos = jnp.arange(size)
    causal = pos[:, None] >= pos[None, :]
    diff = cum[:, :, None] - cum[:, None, :]
    weight = jnp.where(causal[None], jnp.exp(jnp.minimum(diff, 0.0)), 0.0)
    scores = jnp.einsum("thd,shd->hts", qb, kb, preferred_element_type=jnp.float32)
    probs = (scores * weight).astype(jnp.bfloat16)
    intra = jnp.einsum("hts,shd->thd", probs, vb, preferred_element_type=jnp.float32)
    inter = jnp.einsum(
        "thd,hde->the", qb, state.astype(jnp.bfloat16), preferred_element_type=jnp.float32
    )
    return intra + jnp.exp(cum).T[:, :, None] * inter


def join_states(earlier, later):
    return (later[0], jnp.exp(later[0])[:, None, None] * earlier[1] + later[1])


def lightning_part(lin_q, lin_k, lin_v, log_decay, lin_gain):
    tok, width = lin_q.shape
    heads = log_decay.shape[0]
    dim = width // heads
    q = lin_q.reshape(tok, heads, dim)
    k = lin_k.reshape(tok, heads, dim)
    v = lin_v.reshape(tok, heads, dim)
    total = (jnp.zeros((heads,), jnp.float32), jnp.zeros((heads, dim, dim), jnp.float32))
    cum, keys_scaled = block_local(k, log_decay)
    local = jnp.einsum("shd,she->hde", keys_scaled, v, preferred_element_type=jnp.float32)
    total = join_states(total, (cum[:, -1], local))
    logs = lax.all_gather(total[0][None], "ctx", axis=0, tiled=True)
    mine = lax.axis_index("ctx")
    csum = running_sum(logs.T).T
    before = jnp.sum(jnp.where((jnp.arange(logs.shape[0]) < mine)[:, None], logs, 0.0), axis=0)
    piece = lax.all_gather(total[1][None].astype(jnp.bfloat16), "ctx", axis=0, tiled=True).astype(
        jnp.float32
    )
    rows = piece.shape[0]
    idx = jnp.arange(rows)
    live = (idx < mine)[:, None]
    decay_factor = jnp.exp(jnp.where(live, before[None] - csum, -jnp.inf))
    state = jnp.zeros((heads, dim, dim), jnp.float32) + jnp.einsum(
        "jh,jhde->hde", decay_factor, piece, precision=lax.Precision.HIGHEST
    )
    mixed = block_output(q, k, v, cum, state)
    rms = jnp.sqrt(jnp.mean(mixed * mixed, axis=-1, keepdims=True) + 1e-05)
    outputs = mixed / rms * lin_gain.reshape(heads, dim)
    return outputs.reshape(tok, width).astype(jnp.bfloat16)


def softmax_part(soft_q, soft_kv, dim):
    local_q, local_kv = (
        lax.all_to_all(soft_q, "head", split_axis=1, concat_axis=0, tiled=True),
        lax.all_to_all(soft_kv, "head", split_axis=1, concat_axis=0, tiled=True),
    )
    tok = local_q.shape[0]
    half = tok // 2
    kvl = local_kv.shape[1] // (2 * dim)
    group = local_q.shape[1] // (dim * kvl)
    mine = lax.axis_index("ctx")
    first_q = local_q[:half]
    second_q = local_q[half:]
    second_start = mine * tok + half
    first_start = mine * tok
    first_pos = first_start + jnp.arange(half)
    second_pos = second_start + jnp.arange(half)
    first_heads = first_q.reshape(half, kvl, group, dim)
    second_heads = second_q.reshape(half, kvl, group, dim)
    scale = dim ** (-0.5)

    def update(carry, queries, qpos, kblock, kstart):
        peak, total, acc = carry
        size = kblock.shape[0]
        pair = kblock.reshape(size, kvl, 2, dim)
        key_matrix = pair[:, :, 0]
        value_rows = pair[:, :, 1]
        kpos = kstart + jnp.arange(size)
        mask = (kpos[None, :] <= qpos[:, None])[None, None]
        scores = (
            jnp.einsum("qngd,knd->ngqk", queries, key_matrix, preferred_element_type=jnp.float32)
            * scale
        )
        scores = jnp.where(mask, scores, -1e30)
        newpeak = jnp.maximum(peak, jnp.max(scores, axis=-1))
        weights = jnp.where(mask, jnp.exp(scores - newpeak[..., None]), 0.0)
        decay_factor = jnp.exp(peak - newpeak)
        total = total * decay_factor + jnp.sum(weights, axis=-1)
        acc = acc * decay_factor[..., None] + jnp.einsum(
            "ngqk,knd->ngqd",
            weights.astype(jnp.bfloat16),
            value_rows,
            preferred_element_type=jnp.float32,
        )
        return (newpeak, total, acc)

    def guarded(carry, queries, qpos, kblock, kstart):
        return update(carry, queries, qpos, kblock, kstart)

    def start_carry():
        return (
            jnp.full((kvl, group, half), -1e30, jnp.float32),
            jnp.zeros((kvl, group, half), jnp.float32),
            jnp.zeros((kvl, group, half, dim), jnp.float32),
        )

    def finish(carry):
        peak, total, acc = carry
        result = acc / total[..., None]
        return result.transpose(2, 0, 1, 3).reshape(half, kvl * group * dim).astype(jnp.bfloat16)

    piece = lax.all_gather(local_kv, "ctx", axis=0, tiled=True)
    rows = piece.shape[0]
    width = math.gcd(rows, 512)

    def step(index, inner):
        kblock = lax.dynamic_slice_in_dim(piece, index * width, width, 0)
        kstart = index * width
        early = guarded(inner[0], first_heads, first_pos, kblock, kstart)
        later = guarded(inner[1], second_heads, second_pos, kblock, kstart)
        return (early, later)

    early, later = lax.fori_loop(0, rows // width, step, (start_carry(), start_carry()))
    first_out = finish(early)
    second_out = finish(later)
    result = jnp.concatenate([first_out, second_out], axis=0)
    return lax.all_to_all(result, "head", split_axis=0, concat_axis=1, tiled=True)


def mixer_kernel(
    nctx, nz, dim,
    lq_in, lk_in, lv_in, ld_in, gain_in, sq, skv,
    lin_out, soft_out,
    kv_all, q_all, st_send, st_recv, tot_send, tot_recv, pre_send, state_in, cum, mix, out_send,
    lq, lk, lv, ld, gain, in_sem, own_sem, kv_ss, kv_rs, q_ss, q_rs, z_ss, z_rs, st_ss, st_rs, tt_ss, tt_rs, pr_ss, pr_rs,
    o_ss, o_rs,
):
    me = lax.axis_index("ctx")
    zme = lax.axis_index("head")
    tok = lq.shape[0]
    heads = ld.shape[0]
    rows = sq.shape[0]
    qw = sq.shape[1] // nctx
    group = qw // dim
    hpo = heads // nctx
    f32, bf16 = jnp.float32, jnp.bfloat16

    def ctx_peer(k):
        return lax.rem(me + k, nctx)

    def z_peer(k):
        return lax.rem(zme + k, nz)

    loads = [
        pltpu.make_async_copy(src, dst, in_sem.at[i])
        for i, (src, dst) in enumerate(
            [(ld_in, ld), (lk_in, lk), (lv_in, lv), (lq_in, lq), (gain_in, gain)]
        )
    ]
    barrier = pltpu.get_barrier_semaphore()
    for k in range(1, nctx):
        pl.semaphore_signal(barrier, inc=1, device_id=(ctx_peer(k), zme), device_id_type=MESH)
    for k in range(1, nz):
        pl.semaphore_signal(barrier, inc=1, device_id=(me, z_peer(k)), device_id_type=MESH)
    for load in loads:
        load.start()
    pl.semaphore_wait(barrier, nctx + nz - 2)

    def remote(src, dst, ss, rs, k, device):
        return pltpu.make_async_remote_copy(
            src_ref=src, dst_ref=dst, send_sem=ss.at[k], recv_sem=rs.at[k],
            device_id=device, device_id_type=MESH,
        )

    def cols(index, width):
        return pl.ds(pl.multiple_of(index * width, width), width)

    def kv_copy(k):
        d = ctx_peer(k)
        return remote(skv.at[:, cols(d, 2 * dim)], kv_all.at[zme, me], kv_ss, kv_rs, k, (d, zme))

    def q_copy(k):
        d = ctx_peer(k)
        return remote(sq.at[:, cols(d, qw)], q_all.at[me], q_ss, q_rs, k, (d, zme))

    def z_copy(src, step):
        to = jnp.clip(zme + step, 0, nz - 1)
        slot = src if step > 0 else nz + src
        return pltpu.make_async_remote_copy(
            src_ref=kv_all.at[src], dst_ref=kv_all.at[src], send_sem=z_ss.at[slot],
            recv_sem=z_rs.at[src], device_id=(me, to), device_id_type=MESH,
        )

    def z_relay(away):
        @pl.when(zme >= away)
        def _():
            if away > 0:
                z_copy(zme - away, 1).wait_recv()

            @pl.when(zme < nz - 1)
            def _():
                z_copy(zme - away, 1).start()

        @pl.when(zme < nz - away)
        def _():
            if away > 0:
                z_copy(zme + away, -1).wait_recv()

            @pl.when(zme > 0)
            def _():
                z_copy(zme + away, -1).start()

    def st_copy(k):
        d = ctx_peer(k)
        return remote(st_send.at[d], st_recv.at[me], st_ss, st_rs, k, (d, zme))

    def tt_copy(k):
        d = ctx_peer(k)
        return remote(tot_send.at[d], tot_recv.at[me], tt_ss, tt_rs, k, (d, zme))

    def pre_copy(k):
        d = ctx_peer(k)
        return remote(pre_send.at[d], state_in.at[me], pr_ss, pr_rs, k, (d, zme))

    def out_copy(d, k):
        return remote(out_send.at[d], soft_out.at[:, cols(me, qw)], o_ss, o_rs, k, (d, zme))

    own_kv = pltpu.make_async_copy(skv.at[:, cols(me, 2 * dim)], kv_all.at[zme, me], own_sem.at[0])
    own_q = pltpu.make_async_copy(sq.at[:, cols(me, qw)], q_all.at[me], own_sem.at[1])
    own_out = pltpu.make_async_copy(
        out_send.at[me], soft_out.at[:, cols(me, qw)], own_sem.at[2]
    )
    own_kv.start()
    for k in range(1, nctx):
        kv_copy(k).start()

    low = lax.broadcasted_iota(jnp.int32, (tok, tok), 1) <= lax.broadcasted_iota(
        jnp.int32, (tok, tok), 0
    )
    tri = jnp.where(low, 1.0, 0.0).astype(bf16)

    def running(part, wide):
        return lax.dot_general(tri, part, (((1,), (1,)), ((), ())), preferred_element_type=f32)

    def local_state(j, carry):
        for r in range(hpo):
            h = j * hpo + r
            g = jnp.broadcast_to(ld[pl.ds(h, 1), :], (dim, tok))
            g0 = g.astype(bf16)
            rest = g - g0.astype(f32)
            g1 = rest.astype(bf16)
            g2 = (rest - g1.astype(f32)).astype(bf16)
            c = running(g0, dim) + running(g1, dim) + running(g2, dim)
            cum[h] = c
            last = c[tok - 1 : tok, :]
            tot_send[j, pl.ds(r, 1), :] = last
            ks = (lk[:, cols(h, dim)].astype(f32) * jnp.exp(last - c)).astype(bf16)
            st_send[j, r] = lax.dot_general(
                ks, lv[:, cols(h, dim)], (((0,), (0,)), ((), ())), preferred_element_type=f32
            ).astype(bf16)
        return carry

    tot_send[...] = jnp.zeros_like(tot_send)
    for load in loads:
        load.wait()
    lax.fori_loop(0, nctx, local_state, 0)

    own_kv.wait()
    for k in range(1, nctx):
        kv_copy(k).wait_recv()
    z_relay(0)
    for k in range(1, nctx):
        st_copy(k).start()
        tt_copy(k).start()
    own_q.start()
    for k in range(1, nctx):
        q_copy(k).start()
    st_recv[me] = st_send[me]
    tot_recv[me] = tot_send[me]

    def intra(h, carry):
        c = cum[h]
        wide = jnp.concatenate([c] * (tok // dim), axis=1)
        row = jnp.transpose(c)[0:1, :]
        weight = jnp.where(low, jnp.exp(jnp.minimum(wide - row, 0.0)), 0.0)
        s = lax.dot_general(
            lq[:, cols(h, dim)], lk[:, cols(h, dim)], (((1,), (1,)), ((), ())),
            preferred_element_type=f32,
        )
        probs = (s * weight).astype(bf16)
        mix[h] = jnp.dot(probs, lv[:, cols(h, dim)], preferred_element_type=f32)
        return carry

    for part in range(1, nz):
        lax.fori_loop(heads * (part - 1) // (nz - 1), heads * part // (nz - 1), intra, 0)
        if part < nz - 1:
            z_relay(part)

    for k in range(1, nctx):
        st_copy(k).wait_recv()
        tt_copy(k).wait_recv()
    state = [jnp.zeros((dim, dim), f32) for _ in range(hpo)]
    for c in range(nctx):
        for r in range(hpo):
            pre_send[c, r] = state[r].astype(bf16)
            decay = jnp.exp(tot_recv[c, r : r + 1, :])
            state[r] = decay * state[r] + st_recv[c, r].astype(f32)
    for k in range(1, nctx):
        pre_copy(k).start()
    state_in[me] = pre_send[me]

    own_q.wait()
    for k in range(1, nctx):
        q_copy(k).wait_recv()
    z_relay(nz - 1)
    factor = dim ** (-0.5) * math.log2(math.e)
    per = max(1, min(group, tok // rows))
    def attend(c):
        for t in range(group // per):
            q = jnp.concatenate(
                [
                    q_all[c, :, (t * per + i) * dim : (t * per + i + 1) * dim]
                    for i in range(per)
                ],
                axis=0,
            )
            kd = kv_all[:, c, :, :dim].reshape(nz * rows, dim)
            vd = kv_all[:, c, :, dim:].reshape(nz * rows, dim)
            sd = lax.dot_general(q, kd, (((1,), (1,)), ((), ())), preferred_element_type=f32)
            kpos = lax.broadcasted_iota(jnp.int32, sd.shape, 1)
            qpos = zme * rows + lax.rem(lax.broadcasted_iota(jnp.int32, sd.shape, 0), rows)
            sd = jnp.where(kpos <= qpos, sd, -1e30)
            peak = jnp.max(sd, axis=1, keepdims=True)
            if c > 0:
                kp = kv_all[:, :c, :, :dim].reshape(nz * c * rows, dim)
                vp = kv_all[:, :c, :, dim:].reshape(nz * c * rows, dim)
                sp = lax.dot_general(q, kp, (((1,), (1,)), ((), ())), preferred_element_type=f32)
                peak = jnp.maximum(peak, jnp.max(sp, axis=1, keepdims=True))
            wd = jnp.exp2((sd - peak) * factor)
            total = jnp.sum(wd, axis=1, keepdims=True)
            acc = jnp.dot(wd.astype(bf16), vd, preferred_element_type=f32)
            if c > 0:
                wp = jnp.exp2((sp - peak) * factor)
                total = total + jnp.sum(wp, axis=1, keepdims=True)
                acc = acc + jnp.dot(wp.astype(bf16), vp, preferred_element_type=f32)
            out = (acc / total).astype(bf16)
            for i in range(per):
                out_send[c, :, (t * per + i) * dim : (t * per + i + 1) * dim] = out[
                    i * rows : (i + 1) * rows
                ]

    def turn(k, carry):
        c = ctx_peer(k)
        lax.switch(c, [functools.partial(attend, i) for i in range(nctx)])

        @pl.when(k == nctx)
        def _():
            own_out.start()

        @pl.when(k < nctx)
        def _():
            out_copy(c, k).start()

        return carry

    lax.fori_loop(1, nctx + 1, turn, 0)

    for k in range(1, nctx):
        pre_copy(k).wait_recv()

    def finish(j, carry):
        for r in range(hpo):
            h = j * hpo + r
            inter = jnp.dot(lq[:, cols(h, dim)], state_in[j, r], preferred_element_type=f32)
            m = mix[h] + jnp.exp(cum[h]) * inter
            ms = jnp.mean(m * m, axis=1, keepdims=True)
            lin_out[:, cols(h, dim)] = (
                m * lax.rsqrt(ms + 1e-05) * gain[:, cols(h, dim)]
            ).astype(bf16)
        return carry

    lax.fori_loop(0, nctx, finish, 0)

    own_out.wait()
    for k in range(1, nctx):
        out_copy(ctx_peer(k), k).wait()
        kv_copy(k).wait_send()
        q_copy(k).wait_send()
        st_copy(k).wait_send()
        tt_copy(k).wait_send()
        pre_copy(k).wait_send()
    for away in range(nz):

        @pl.when((zme >= away) & (zme < nz - 1))
        def _(away=away):
            z_copy(zme - away, 1).wait_send()

        @pl.when((zme < nz - away) & (zme > 0))
        def _(away=away):
            z_copy(zme + away, -1).wait_send()


def fused_body(nctx, nz, lin_q, lin_k, lin_v, log_decay, lin_gain, soft_q, soft_kv):
    tok, width = lin_q.shape
    heads = log_decay.shape[0]
    dim = width // heads
    rows = soft_q.shape[0]
    qw = soft_q.shape[1] // nctx
    hpo = heads // nctx
    f32, bf16 = jnp.float32, jnp.bfloat16
    vmem = pl.BlockSpec(memory_space=pltpu.VMEM)
    hbm = pl.BlockSpec(memory_space=pltpu.HBM)
    anywhere = pl.BlockSpec(memory_space=pl.ANY)
    dma = pltpu.SemaphoreType.DMA
    return pl.pallas_call(
        functools.partial(mixer_kernel, nctx, nz, dim),
        out_shape=(
            jax.ShapeDtypeStruct(lin_q.shape, bf16),
            jax.ShapeDtypeStruct(soft_q.shape, bf16),
        ),
        in_specs=[hbm] * 7,
        out_specs=(vmem, anywhere),
        scratch_shapes=[
            pltpu.VMEM((nz, nctx, rows, 2 * dim), bf16),
            pltpu.VMEM((nctx, rows, qw), bf16),
            pltpu.VMEM((nctx, hpo, dim, dim), bf16),
            pltpu.VMEM((nctx, hpo, dim, dim), bf16),
            pltpu.VMEM((nctx, 8, dim), f32),
            pltpu.VMEM((nctx, 8, dim), f32),
            pltpu.VMEM((nctx, hpo, dim, dim), bf16),
            pltpu.VMEM((nctx, hpo, dim, dim), bf16),
            pltpu.VMEM((heads, tok, dim), f32),
            pltpu.VMEM((heads, tok, dim), f32),
            pltpu.VMEM((nctx, rows, qw), bf16),
            pltpu.VMEM(lin_q.shape, bf16),
            pltpu.VMEM(lin_q.shape, bf16),
            pltpu.VMEM(lin_q.shape, bf16),
            pltpu.VMEM(log_decay.shape, f32),
            pltpu.VMEM((1, width), f32),
            dma((5,)),
            dma((3,)),
            dma((nctx,)), dma((nctx,)),
            dma((nctx,)), dma((nctx,)),
            dma((2 * nz,)), dma((nz,)),
            dma((nctx,)), dma((nctx,)),
            dma((nctx,)), dma((nctx,)),
            dma((nctx,)), dma((nctx,)),
            dma((nctx,)), dma((nctx,)),
        ],
        compiler_params=pltpu.CompilerParams(
            collective_id=0, has_side_effects=True, vmem_limit_bytes=50 * 1024 * 1024
        ),
        cost_estimate=pl.CostEstimate(
            flops=4 * 10**9, bytes_accessed=8 * 10**6, transcendentals=6 * 10**6
        ),
        name="mixers",
    )(lin_q, lin_k, lin_v, log_decay, lin_gain.reshape(1, width), soft_q, soft_kv)


def body(nctx, nz, lin_q, lin_k, lin_v, log_decay, lin_gain, soft_q, soft_kv):
    heads = log_decay.shape[0]
    dim = lin_q.shape[1] // heads
    kv_heads = soft_kv.shape[1] // (2 * dim)
    if kv_heads == nctx and heads % nctx == 0 and heads // nctx <= 8:
        return fused_body(
            nctx, nz, lin_q, lin_k, lin_v, log_decay, lin_gain, soft_q, soft_kv
        )
    lin_out = lightning_part(lin_q, lin_k, lin_v, log_decay, lin_gain)
    soft_out = softmax_part(soft_q, soft_kv, dim)
    return (lin_out, soft_out)


def solution(mesh):
    return jax.shard_map(
        functools.partial(body, mesh.shape["ctx"], mesh.shape["head"]),
        mesh=mesh,
        in_specs=(
            P("ctx", "head"),
            P("ctx", "head"),
            P("ctx", "head"),
            P("head", "ctx"),
            P("head"),
            P(("ctx", "head"), None),
            P(("ctx", "head"), None),
        ),
        out_specs=(P("ctx", "head"), P(("ctx", "head"), None)),
        check_vma=False,
    )
```
